32 devices in a mesh: row: 8 (over y, x, core), col: 4 (over z).
Axes of the slice: x: 2, y: 2, z: 4, core: 2. Of those that a mesh axis runs over, the one named last changes fastest.
Arguments:
- tiles: bfloat16 [2, 16384, 8192], P(None, 'row', 'col'), may hold values from -0.0625 to 0.0625
- probe: bfloat16 [2, 16384, 256], P(None, ('row', 'col')), may hold values from -6 to 6
- cluster_perm: int32 [2, 8, 2048], P(None, 'row'), may hold values from 0 to 2047, each once within a row
- tile_keep: int32 [2, 8, 4], P(None, 'row', 'col'), may hold values 0 or 1
Outputs:
- samples: float32 [2, 16384, 256], P(None, ('row', 'col'))
- leaf_basis: float32 [2, 16384, 256], P(None, ('row', 'col'))
The draws below stay inside these ranges and needn't reach their ends.
Inputs may be any that keep to these rules, and one draw needn't show every extreme that they name: Each row of cluster_perm is a permutation. `tile_keep`: entries with c = 0 are not read.
All inputs are finite; a program needn't handle non-finite values. No bound on the sum of `tile_keep` on one device may be relied on, other than what follows from the above.
Results may differ from the reference program's by a relative error of at most 0.0003.
Values may be sent and summed in bfloat16 or wider, within the bound.
A program may use at most 128 MiB of HBM per device.

```python
import jax
import jax.numpy as jnp
from jax import lax

TILE = 2048
P_SIZE = 256
CPR = 2
NCL = 16
N_ROW = 8
N_COL = 4


def plant(array, rng, low, largest):
    index_at = [jax.random.randint(jax.random.fold_in(rng, axis), (), 0, length) for axis, length in enumerate(array.shape)]
    longest = array.shape.index(max(array.shape))
    next_to = index_at[:longest] + [(index_at[longest] + 1) % array.shape[longest]] + index_at[longest + 1:]
    return array.at[tuple(index_at)].set(low).at[tuple(next_to)].set(largest)


def block_levels(stream_key, extent, shards, low, top_value):
    def one(axis_at, blocks):
        heights = jax.random.uniform(jax.random.fold_in(jax.random.fold_in(stream_key, 6), axis_at), (blocks,), jnp.float32, low / len(shards), top_value / len(shards))
        return jnp.repeat(jnp.exp(heights), extent[axis_at] // blocks).reshape((-1,) + (1,) * (len(extent) - axis_at - 1))

    loudness = one(*shards[0])
    for cut in shards[1:]:
        loudness = loudness * one(*cut)
    return loudness


def normal_values(key, dims, width, most, cuts=(), dtype=jnp.bfloat16):
    values = jax.random.normal(key, dims, jnp.float32) * width
    if len(cuts) > 0:
        values = block_levels(key, dims, cuts, -0.22, 0.18) * values
    return jnp.clip(values, min=-most, max=most).astype(dtype)


def setup_inputs(seed: int = 0) -> dict:
    splits = jax.random.split(jax.random.key(seed), 5)
    tiles = normal_values(splits[0], (CPR, N_ROW * TILE, N_COL * TILE), (N_COL * TILE) ** -0.5, 0.0625, ((1, 8), (2, 4)))
    probe = normal_values(splits[1], (CPR, N_ROW * TILE, P_SIZE), 1.0, 6.0, ((1, 32),))
    cluster_perm = jax.vmap(lambda own: jax.random.permutation(own, TILE))(jax.random.split(splits[2], CPR * N_ROW)).reshape((CPR, N_ROW, TILE)).astype(jnp.int32)
    tile_keep = plant((jax.random.randint(splits[3], (CPR, N_ROW, N_COL), 0, 4) < 3).astype(jnp.int32), jax.random.fold_in(splits[3], 1), 0, 1)
    return {"tiles": tiles, "probe": probe, "cluster_perm": cluster_perm, "tile_keep": tile_keep}


def reference(tiles, probe, cluster_perm, tile_keep):
    grouped = probe.reshape(CPR, N_ROW, TILE, P_SIZE)
    order = cluster_perm.astype(jnp.int32)[:, :, :, None]
    omega = jnp.take_along_axis(grouped, order, axis=2).reshape(NCL, TILE, P_SIZE)
    keep_flags = tile_keep.astype(jnp.float32)
    partial_value = [jnp.zeros((TILE, P_SIZE), jnp.float32) for index in range(NCL)]
    for slot in range(CPR):
        for row_cl in range(N_ROW):
            first = slot * N_ROW + row_cl
            for offset in range(N_COL):
                second = (first + offset) % NCL
                tile_block = tiles[slot, row_cl * TILE:(row_cl + 1) * TILE, offset * TILE:(offset + 1) * TILE]
                weight = 0.5 if offset == 0 else keep_flags[slot, row_cl, offset]
                forward = jnp.dot(tile_block.astype(jnp.float32), omega[second].astype(jnp.float32), preferred_element_type=jnp.float32)
                backward = lax.dot_general(tile_block.astype(jnp.float32), omega[first].astype(jnp.float32), (((0,), (0,)), ((), ())), preferred_element_type=jnp.float32)
                partial_value[first] = partial_value[first] + weight * forward
                partial_value[second] = partial_value[second] + weight * backward
    blocks = jnp.stack(partial_value, 0)

    def orthogonal(block):
        gram_sum = jnp.dot(block.T, block, precision=lax.Precision.HIGHEST) / TILE
        factor = jnp.linalg.cholesky(gram_sum)
        return jax.scipy.linalg.solve_triangular(factor, block.T, lower=True).T
    bases = jax.vmap(orthogonal)(blocks)
    return (blocks.reshape(CPR, N_ROW * TILE, P_SIZE), bases.reshape(CPR, N_ROW * TILE, P_SIZE))
```

```python
import functools

import jax
import jax.numpy as jnp
from jax import lax
from jax.experimental import pallas as pl
from jax.experimental.pallas import tpu as pltpu
from jax.sharding import PartitionSpec as P

HIGHEST = lax.Precision.HIGHEST
LIMIT = 56 * 1024 * 1024
STEP = 256
NB = 64
AB_T = (((1,), (1,)), ((), ()))
AT_B = (((0,), (0,)), ((), ()))


def sort_rows(raw_ref, perm_ref, out_ref, slot):
    rows = out_ref.shape[1]
    points = raw_ref.shape[1]

    def block(index, carry):
        at = pl.multiple_of(index * STEP, STEP)
        order = perm_ref[slot, :, pl.ds(at, STEP)]
        order = jnp.broadcast_to(order, (128, STEP)).T
        total = jnp.zeros((STEP, out_ref.shape[2]), jnp.float32)
        pieces = []
        for lane in range(0, points, 128):
            column = lax.broadcasted_iota(jnp.int32, (STEP, 128), 1) + lane
            pieces.append(jnp.where(order == column, 1.0, 0.0).astype(jnp.bfloat16))
        hot = jnp.concatenate(pieces, axis=1)
        total = jnp.dot(hot, raw_ref[slot], preferred_element_type=jnp.float32)
        out_ref[slot, pl.ds(at, STEP), :] = total.astype(out_ref.dtype)
        return carry

    lax.fori_loop(0, rows // STEP, block, 0)


def sort_kernel(raw_ref, perm_ref, out_ref):
    for slot in range(out_ref.shape[0]):
        sort_rows(raw_ref, perm_ref, out_ref, slot)


def encode(value):
    top = jnp.max(jnp.abs(value), axis=1, keepdims=True)
    scale = jnp.where(top > 0.0, top, 1.0) * (1.0 / 32766.0)
    code = jnp.round(value * (1.0 / scale)).astype(jnp.int32).astype(jnp.int16)
    return code, scale


def backward_kernel(weight_ref, tiles_ref, omega_ref, code_ref, scale_ref):
    slot = pl.program_id(0)
    weight = weight_ref[slot]
    omega_t = omega_ref[0].T

    def block(index, carry):
        at = pl.multiple_of(index * STEP, STEP)
        value = jnp.dot(omega_t, tiles_ref[0, :, pl.ds(at, STEP)], preferred_element_type=jnp.float32)
        code, scale = encode(value.T * weight)
        code_ref[0, pl.ds(at, STEP), :] = code
        scale_ref[0, :, pl.ds(at, STEP)] = jnp.broadcast_to(scale, (STEP, 128)).T[0:1]
        return carry

    lax.fori_loop(0, code_ref.shape[1] // STEP, block, 0)


def forward_kernel(weight_ref, tiles_ref, far_ref, code_ref, scale_ref, out_ref):
    slot = pl.program_id(0)
    weight = weight_ref[slot]

    def block(index, carry):
        at = pl.multiple_of(index * STEP, STEP)
        value = jnp.dot(tiles_ref[0, pl.ds(at, STEP), :], far_ref[0], preferred_element_type=jnp.float32)
        scale = jnp.broadcast_to(scale_ref[0, :, pl.ds(at, STEP)], (128, STEP)).T
        code = code_ref[0, pl.ds(at, STEP), :].astype(jnp.int32).astype(jnp.float32)
        other = jnp.concatenate([code[:, lane:lane + 128] * scale for lane in range(0, code.shape[1], 128)], axis=1)
        out_ref[0, pl.ds(at, STEP), :] = value * weight + other
        return carry

    lax.fori_loop(0, out_ref.shape[1] // STEP, block, 0)


def eliminate(squares):
    parts = NB // 8
    row_at = lax.broadcasted_iota(jnp.int32, (8, 128), 0)
    lane_at = lax.broadcasted_iota(jnp.int32, (8, 128), 1)
    work = [[square[8 * t:8 * t + 8, :] for t in range(parts)] for square in squares]
    unit = [[jnp.where(row_at + 8 * t == lane_at, 1.0, 0.0) for t in range(parts)] for _ in squares]
    for j in range(NB):
        top, row = j // 8, j % 8
        for b in range(len(squares)):
            left, right = work[b][top][row:row + 1, :], unit[b][top][row:row + 1, :]
            inverse = 1.0 / left[:, j:j + 1]
            left_scaled, right_scaled = left * inverse, right * inverse
            for t in range(top, parts):
                factor = work[b][t][:, j:j + 1]
                if t == top:
                    factor = jnp.where(row_at[:, :1] > row, factor, 0.0)
                work[b][t] = work[b][t] - factor * left_scaled
                unit[b][t] = unit[b][t] - factor * right_scaled
    inverses = []
    for b in range(len(squares)):
        scaled = []
        for t in range(parts):
            pivot = jnp.sum(jnp.where(row_at + 8 * t == lane_at, work[b][t], 0.0), axis=1, keepdims=True)
            scaled.append(unit[b][t] * lax.rsqrt(pivot))
        inverses.append(jnp.concatenate(scaled, axis=0)[:, :NB])
    return inverses


def invert_factors(gram_ref, unit_ref, inverse_ref):
    slots, size = gram_ref.shape[0], gram_ref.shape[1]
    row_at = lax.broadcasted_iota(jnp.int32, (size, size), 0)
    lane_at = lax.broadcasted_iota(jnp.int32, (size, size), 1)
    for k in range(slots):
        unit_ref[k] = jnp.where(row_at == lane_at, 1.0, 0.0)

    def panel(index, carry):
        inverses = eliminate([gram_ref[k, 0:NB, 0:128] for k in range(slots)])
        for k in range(slots):
            across = jnp.dot(inverses[k], gram_ref[k, 0:NB, :], precision=HIGHEST, preferred_element_type=jnp.float32)
            done = jnp.dot(inverses[k], unit_ref[k, 0:NB, :], precision=HIGHEST, preferred_element_type=jnp.float32)
            inverse_ref[k, pl.ds(pl.multiple_of(index * NB, NB), NB), :] = done
            across_t = across.T[NB:, :]
            less = jnp.dot(across_t, across, precision=HIGHEST, preferred_element_type=jnp.float32)
            gram_ref[k, 0:size - NB, :] = pltpu.roll(gram_ref[k, NB:, :] - less, size - NB, 1)
            less = jnp.dot(across_t, done, precision=HIGHEST, preferred_element_type=jnp.float32)
            unit_ref[k, 0:size - NB, :] = unit_ref[k, NB:, :] - less
        return carry

    lax.fori_loop(0, size // NB, panel, 0)


def basis_kernel(points, samples_ref, gram_ref, basis_ref, work_ref, unit_ref, inverse_ref):
    work_ref[...] = gram_ref[...] * (1.0 / points)
    invert_factors(work_ref, unit_ref, inverse_ref)
    for k in range(samples_ref.shape[0]):
        basis_ref[k] = lax.dot_general(
            samples_ref[k], inverse_ref[k], AB_T, precision=HIGHEST, preferred_element_type=jnp.float32
        )


def per_device(tiles, probe, cluster_perm, tile_keep):
    row_id = lax.axis_index("row")
    col_id = lax.axis_index("col")
    nrows = lax.axis_size("row")
    ncols = lax.axis_size("col")
    slots, points, _ = tiles.shape
    width = probe.shape[2]
    params = pltpu.CompilerParams(vmem_limit_bytes=LIMIT)
    whole = pl.BlockSpec(memory_space=pltpu.VMEM)
    scalar = pl.BlockSpec(memory_space=pltpu.SMEM)

    def slot_block(rows, cols):
        return pl.BlockSpec((1, rows, cols), lambda k: (k, 0, 0))

    def shifted(value, sign):
        pairs = [
            (r * ncols + c, (r + sign * c) % nrows * ncols + c) for r in range(nrows) for c in range(ncols)
        ]
        return lax.ppermute(value, ("row", "col"), pairs)

    weight = jnp.where(col_id == 0, 0.5, tile_keep[:, 0, 0].astype(jnp.float32))
    raw = lax.all_gather(probe, "col", axis=1, tiled=True)
    omega = pl.pallas_call(
        sort_kernel,
        out_shape=jax.ShapeDtypeStruct((slots, points, width), jnp.bfloat16),
        in_specs=[whole, whole],
        out_specs=whole,
        compiler_params=params,
        name="sort_rows",
    )(raw, cluster_perm)
    far = shifted(omega, -1)
    code, scale = pl.pallas_call(
        backward_kernel,
        grid=(slots,),
        out_shape=(
            jax.ShapeDtypeStruct((slots, points, width), jnp.int16),
            jax.ShapeDtypeStruct((slots, 1, points), jnp.float32),
        ),
        in_specs=[scalar, slot_block(points, points), slot_block(points, width)],
        out_specs=(slot_block(points, width), slot_block(1, points)),
        compiler_params=params,
        cost_estimate=pl.CostEstimate(flops=4 * points * points * width, bytes_accessed=2 * tiles.size, transcendentals=0),
        name="backward_products",
    )(weight, tiles, omega)
    code, scale = shifted(code, 1), shifted(scale, 1)
    take_far = (row_id + col_id >= nrows).astype(jnp.int32)
    take_near = (row_id < col_id).astype(jnp.int32)
    selects = jnp.stack([take_far, take_near])

    def far_block(k, sel):
        return ((k + sel[0]) % slots, 0, 0)

    def near_block(k, sel):
        return ((k + slots - sel[1]) % slots, 0, 0)

    def plain_block(k, sel):
        return (k, 0, 0)

    combined = pl.pallas_call(
        lambda sel, *refs: forward_kernel(*refs),
        grid_spec=pltpu.PrefetchScalarGridSpec(
            num_scalar_prefetch=1,
            grid=(slots,),
            in_specs=[
                scalar,
                pl.BlockSpec((1, points, points), plain_block),
                pl.BlockSpec((1, points, width), far_block),
                pl.BlockSpec((1, points, width), near_block),
                pl.BlockSpec((1, 1, points), near_block),
            ],
            out_specs=pl.BlockSpec((1, points, width), plain_block),
        ),
        out_shape=jax.ShapeDtypeStruct((slots, points, width), jnp.float32),
        compiler_params=params,
        cost_estimate=pl.CostEstimate(flops=4 * points * points * width, bytes_accessed=2 * tiles.size, transcendentals=0),
        name="forward_products",
    )(selects, weight, tiles, far, code, scale)
    samples = lax.psum_scatter(combined, "col", scatter_dimension=1, tiled=True)
    local_gram = jnp.einsum("kip,kiq->kpq", samples, samples, precision=HIGHEST)
    gram_sum = lax.psum(local_gram, "col")
    square = pltpu.VMEM((slots, width, width), jnp.float32)
    leaf_basis = pl.pallas_call(
        functools.partial(basis_kernel, points),
        out_shape=jax.ShapeDtypeStruct(samples.shape, jnp.float32),
        in_specs=[whole, whole],
        out_specs=whole,
        scratch_shapes=[square, square, square],
        compiler_params=params,
        name="leaf_basis",
    )(samples, gram_sum)
    return (samples, leaf_basis)


def solution(mesh):
    placed = (
        P(None, "row", "col"),
        P(None, ("row", "col"), None),
        P(None, "row", None),
        P(None, "row", "col"),
    )
    return jax.shard_map(
        per_device,
        mesh=mesh,
        in_specs=placed,
        out_specs=(P(None, ("row", "col"), None), P(None, ("row", "col"), None)),
        check_vma=False,
    )
```

```python
import functools

import jax
import jax.numpy as jnp
from jax import lax
from jax.experimental import pallas as pl
from jax.experimental.pallas import tpu as pltpu
from jax.sharding import PartitionSpec as P

HIGHEST = lax.Precision.HIGHEST
LIMIT = 56 * 1024 * 1024
STEP = 256
NB = 64
AB_T = (((1,), (1,)), ((), ()))
AT_B = (((0,), (0,)), ((), ()))


def sort_rows(raw_ref, perm_ref, out_ref, slot):
    rows, width = out_ref.shape[1:]
    parts, per = raw_ref.shape[1:3]

    def block(index, carry):
        at = pl.multiple_of(index * STEP, STEP)
        order = jnp.broadcast_to(perm_ref[slot, :, pl.ds(at, STEP)], (128, STEP)).T
        total = jnp.zeros((STEP, width), jnp.float32)
        for part in range(parts):
            pieces = []
            for lane in range(part * per, part * per + per, 128):
                column = lax.broadcasted_iota(jnp.int32, (STEP, 128), 1) + lane
                pieces.append(jnp.where(order == column, 1.0, 0.0).astype(jnp.bfloat16))
            hot = jnp.concatenate(pieces, axis=1)
            total = total + jnp.dot(hot, raw_ref[slot, part], preferred_element_type=jnp.float32)
        out_ref[slot, pl.ds(at, STEP), :] = total.astype(out_ref.dtype)
        return carry

    lax.fori_loop(0, rows // STEP, block, 0)


def encode(value):
    top = jnp.max(jnp.abs(value), axis=1, keepdims=True)
    scale = jnp.where(top > 0.0, top, 1.0) * (1.0 / 32766.0)
    code = jnp.round(value * (1.0 / scale)).astype(jnp.int32).astype(jnp.int16)
    return code, scale


def decode(code, scale):
    value = code.astype(jnp.int32).astype(jnp.float32)
    scale = jnp.broadcast_to(scale, (128, scale.shape[1])).T
    return jnp.concatenate([value[:, lane:lane + 128] * scale for lane in range(0, value.shape[1], 128)], axis=1)


def as_lanes(scale):
    return jnp.broadcast_to(scale, (scale.shape[0], 128)).T[0:1]


def samples_kernel(
    nrows, n, weight_ref, tiles_ref, probe_ref, perm_ref, samples_ref, gram_ref,
    tile, raw, omega, far, back_code, back_scale, near_code, near_scale,
    combined, code, scale, got_code, got_scale, part_gram, got_gram,
    tile_sem, hop_send, hop_recv, far_send, far_recv, back_send, back_recv, own_send, own_recv, gram_send, gram_recv,
):
    slots, points, width = omega.shape
    per = points // n
    half = width // 2
    row, me = lax.axis_index("row"), lax.axis_index("col")
    before, after = lax.rem(row + nrows - me, nrows), lax.rem(row + me, nrows)
    from_wrap = jnp.where(row < me, 1, 0)
    to_wrap = jnp.where(row + me >= nrows, 1, 0)
    others = [lax.rem(me + o, n) for o in range(1, n)]
    mesh_id = pl.DeviceIdType.MESH

    def remote(src, dst, send, recv, where):
        return pltpu.make_async_remote_copy(
            src_ref=src, dst_ref=dst, send_sem=send, recv_sem=recv, device_id=where, device_id_type=mesh_id
        )

    def tile_copy(k):
        return pltpu.make_async_copy(tiles_ref.at[k], tile.at[k], tile_sem.at[k])

    def inside(at):
        return (at >= 0) & (at < n)

    def hop(k, side, s, block):
        step = 1 - 2 * side
        to = jnp.where(inside(me + step), me + step, me - step)
        src = probe_ref.at[k] if s == 0 else raw.at[k, block]
        return remote(src, raw.at[k, block], hop_send.at[k, side, s], hop_recv.at[k, side, s], {"col": to})

    def relay(k, s):
        for side in range(2):
            step = 1 - 2 * side
            block = me - s * step

            @pl.when(inside(block))
            def _():
                hop(k, side, s - 1, block).wait_recv()

            if s < n - 1:

                @pl.when(inside(block) & inside(me + step))
                def _():
                    hop(k, side, s, block).start()

    def far_copy(k):
        slot = lax.rem(k - from_wrap + slots, slots)
        return remote(omega.at[k], far.at[slot], far_send.at[k], far_recv.at[slot], {"row": before})

    def far_wait(slot):
        remote(omega.at[slot], far.at[slot], far_send.at[slot], far_recv.at[slot], {"row": before}).wait_recv()

    def back_copies(k, slot):
        return (
            remote(back_code.at[k], near_code.at[slot], back_send.at[k, 0], back_recv.at[slot, 0], {"row": after}),
            remote(back_scale.at[k], near_scale.at[slot], back_send.at[k, 1], back_recv.at[slot, 1], {"row": after}),
        )

    def own_copies(k, o):
        to = others[o]
        return (
            remote(code.at[k, to], got_code.at[k, o], own_send.at[k, o, 0], own_recv.at[k, o, 0], {"col": to}),
            remote(scale.at[k, to], got_scale.at[k, o], own_send.at[k, o, 1], own_recv.at[k, o, 1], {"col": to}),
        )

    def gram_copy(k, o):
        return remote(part_gram.at[k], got_gram.at[k, o], gram_send.at[k, o], gram_recv.at[k, o], {"col": others[o]})

    def sort_and_send(k):
        sort_rows(raw, perm_ref, omega, k)

        @pl.when(me > 0)
        def _():
            far_copy(k).start()

    def backward(k):
        omega_t = omega[k].T

        def block(index, carry):
            at = pl.multiple_of(index * STEP, STEP)
            value = jnp.dot(omega_t, tile[k, :, pl.ds(at, STEP)], preferred_element_type=jnp.float32)
            coded, scales = encode(value.T * weight_ref[k])
            back_code[k, pl.ds(at, STEP), :] = coded
            back_scale[k, :, pl.ds(at, STEP)] = as_lanes(scales)
            return carry

        lax.fori_loop(0, points // STEP, block, 0)

        @pl.when(me > 0)
        def _():
            for copy in back_copies(k, lax.rem(k + to_wrap, slots)):
                copy.start()

    def forward(k):

        @pl.when(me > 0)
        def _():
            far_wait(k)

        @pl.when(me == 0)
        def _():
            far[k] = omega[k]

        def block(index, carry):
            at = pl.multiple_of(index * per, per)
            value = jnp.dot(tile[k, pl.ds(at, per), :], far[k], preferred_element_type=jnp.float32)
            combined[k, index] = value * weight_ref[k]
            return carry

        lax.fori_loop(0, n, block, 0)

    def combine(k):

        @pl.when(me > 0)
        def _():
            for copy in back_copies(k, k):
                copy.wait_recv()

        @pl.when(me == 0)
        def _():
            near_code[k] = back_code[k]
            near_scale[k] = back_scale[k]

        def block(index, carry):
            at = pl.multiple_of(index * per, per)
            value = combined[k, index] + decode(near_code[k, pl.ds(at, per), :], near_scale[k, :, pl.ds(at, per)])
            combined[k, index] = value
            coded, scales = encode(value)
            code[k, index] = coded
            scale[k, index] = as_lanes(scales)
            return carry

        lax.fori_loop(0, n, block, 0)
        for o in range(n - 1):
            for copy in own_copies(k, o):
                copy.start()

    def collect(k):
        total = combined[k, me]
        for o in range(n - 1):
            for copy in own_copies(k, o):
                copy.wait_recv()
            total = total + decode(got_code[k, o], got_scale[k, o])
        samples_ref[k] = total
        total_t = total.T
        upper = jnp.dot(total_t[:half], total, precision=HIGHEST, preferred_element_type=jnp.float32)
        lower = jnp.dot(total_t[half:], total[:, half:], precision=HIGHEST, preferred_element_type=jnp.float32)
        part_gram[k, 0:half] = upper[:, :half]
        part_gram[k, half:2 * half] = upper[:, half:]
        part_gram[k, 2 * half:3 * half] = lower
        for o in range(n - 1):
            gram_copy(k, o).start()

    def gather_gram(k):
        total = part_gram[k]
        for o in range(n - 1):
            gram_copy(k, o).wait_recv()
            total = total + got_gram[k, o]
        gram_ref[k, 0:half, 0:half] = total[0:half]
        gram_ref[k, 0:half, half:] = total[half:2 * half]
        gram_ref[k, half:, 0:half] = total[half:2 * half].T
        gram_ref[k, half:, half:] = total[2 * half:]

    barrier = pltpu.get_barrier_semaphore()
    for to in others:
        pl.semaphore_signal(barrier, inc=1, device_id={"col": to}, device_id_type=mesh_id)

    @pl.when(me > 0)
    def _():
        pl.semaphore_signal(barrier, inc=1, device_id={"row": before}, device_id_type=mesh_id)
        pl.semaphore_signal(barrier, inc=1, device_id={"row": after}, device_id_type=mesh_id)
        pl.semaphore_wait(barrier, n + 1)

    @pl.when(me == 0)
    def _():
        pl.semaphore_wait(barrier, n - 1)

    for k in range(slots):
        for side in range(2):

            @pl.when(inside(me + 1 - 2 * side))
            def _():
                hop(k, side, 0, me).start()

    for k in range(slots):
        tile_copy(k).start()
        raw[k, me] = probe_ref[k]
    for s in range(1, n):
        relay(0, s)
    for k in range(slots):
        if k + 1 < slots:
            relay(k + 1, 1)
        sort_and_send(k)
        if k + 1 < slots:
            for s in range(2, n - 1):
                relay(k + 1, s)
        tile_copy(k).wait()
        backward(k)
        if k + 1 < slots:
            relay(k + 1, n - 1)
    for k in range(slots):
        forward(k)
        combine(k)
    for k in range(slots):
        collect(k)
    for k in range(slots):
        gather_gram(k)

    for k in range(slots):
        for side in range(2):
            step = 1 - 2 * side
            for s in range(n - 1):

                @pl.when(inside(me - s * step) & inside(me + step))
                def _():
                    hop(k, side, s, me - s * step).wait_send()

        @pl.when(me > 0)
        def _():
            far_copy(k).wait_send()
            for copy in back_copies(k, lax.rem(k + to_wrap, slots)):
                copy.wait_send()

        for o in range(n - 1):
            for copy in own_copies(k, o):
                copy.wait_send()
            gram_copy(k, o).wait_send()


def eliminate(squares):
    parts = NB // 8
    row_at = lax.broadcasted_iota(jnp.int32, (8, 128), 0)
    lane_at = lax.broadcasted_iota(jnp.int32, (8, 128), 1)
    work = [[square[8 * t:8 * t + 8, :] for t in range(parts)] for square in squares]
    unit = [[jnp.where(row_at + 8 * t == lane_at, 1.0, 0.0) for t in range(parts)] for _ in squares]
    for j in range(NB):
        top, row = j // 8, j % 8
        for b in range(len(squares)):
            left, right = work[b][top][row:row + 1, :], unit[b][top][row:row + 1, :]
            inverse = 1.0 / left[:, j:j + 1]
            left_scaled, right_scaled = left * inverse, right * inverse
            for t in range(top, parts):
                factor = work[b][t][:, j:j + 1]
                if t == top:
                    factor = jnp.where(row_at[:, :1] > row, factor, 0.0)
                work[b][t] = work[b][t] - factor * left_scaled
                unit[b][t] = unit[b][t] - factor * right_scaled
    inverses = []
    for b in range(len(squares)):
        scaled = []
        for t in range(parts):
            pivot = jnp.sum(jnp.where(row_at + 8 * t == lane_at, work[b][t], 0.0), axis=1, keepdims=True)
            scaled.append(unit[b][t] * lax.rsqrt(pivot))
        inverses.append(jnp.concatenate(scaled, axis=0)[:, :NB])
    return inverses


def invert_factors(gram_ref, unit_ref, inverse_ref):
    slots, size = gram_ref.shape[0], gram_ref.shape[1]
    row_at = lax.broadcasted_iota(jnp.int32, (size, size), 0)
    lane_at = lax.broadcasted_iota(jnp.int32, (size, size), 1)
    for k in range(slots):
        unit_ref[k] = jnp.where(row_at == lane_at, 1.0, 0.0)

    def panel(index, carry):
        inverses = eliminate([gram_ref[k, 0:NB, 0:128] for k in range(slots)])
        for k in range(slots):
            across = jnp.dot(inverses[k], gram_ref[k, 0:NB, :], precision=HIGHEST, preferred_element_type=jnp.float32)
            done = jnp.dot(inverses[k], unit_ref[k, 0:NB, :], precision=HIGHEST, preferred_element_type=jnp.float32)
            inverse_ref[k, pl.ds(pl.multiple_of(index * NB, NB), NB), :] = done
            across_t = across.T[NB:, :]
            less = jnp.dot(across_t, across, precision=HIGHEST, preferred_element_type=jnp.float32)
            gram_ref[k, 0:size - NB, :] = pltpu.roll(gram_ref[k, NB:, :] - less, size - NB, 1)
            less = jnp.dot(across_t, done, precision=HIGHEST, preferred_element_type=jnp.float32)
            unit_ref[k, 0:size - NB, :] = unit_ref[k, NB:, :] - less
        return carry

    lax.fori_loop(0, size // NB, panel, 0)


def basis_kernel(points, samples_ref, gram_ref, basis_ref, work_ref, unit_ref, inverse_ref):
    work_ref[...] = gram_ref[...] * (1.0 / points)
    invert_factors(work_ref, unit_ref, inverse_ref)
    for k in range(samples_ref.shape[0]):
        basis_ref[k] = lax.dot_general(
            samples_ref[k], inverse_ref[k], AB_T, precision=HIGHEST, preferred_element_type=jnp.float32
        )


def per_device(tiles, probe, cluster_perm, tile_keep):
    nrows = lax.axis_size("row")
    ncols = lax.axis_size("col")
    slots, points, _ = tiles.shape
    per, width = probe.shape[1:]
    half = width // 2
    whole = pl.BlockSpec(memory_space=pltpu.VMEM)
    weight = jnp.where(lax.axis_index("col") == 0, 0.5, tile_keep[:, 0, 0].astype(jnp.float32))
    vmem = pltpu.VMEM
    sem = pltpu.SemaphoreType.DMA
    bf16, f32, i16 = jnp.bfloat16, jnp.float32, jnp.int16
    samples, gram_sum = pl.pallas_call(
        functools.partial(samples_kernel, nrows, ncols),
        out_shape=(
            jax.ShapeDtypeStruct((slots, per, width), f32),
            jax.ShapeDtypeStruct((slots, width, width), f32),
        ),
        in_specs=[pl.BlockSpec(memory_space=pltpu.SMEM), pl.BlockSpec(memory_space=pl.ANY), whole, whole],
        out_specs=(whole, whole),
        scratch_shapes=[
            vmem((slots, points, points), bf16),
            vmem((slots, ncols, per, width), bf16),
            vmem((slots, points, width), bf16),
            vmem((slots, points, width), bf16),
            vmem((slots, points, width), i16),
            vmem((slots, 1, points), f32),
            vmem((slots, points, width), i16),
            vmem((slots, 1, points), f32),
            vmem((slots, ncols, per, width), f32),
            vmem((slots, ncols, per, width), i16),
            vmem((slots, ncols, 1, per), f32),
            vmem((slots, ncols - 1, per, width), i16),
            vmem((slots, ncols - 1, 1, per), f32),
            vmem((slots, 3 * half, half), f32),
            vmem((slots, ncols - 1, 3 * half, half), f32),
            sem((slots,)),
            sem((slots, 2, ncols - 1)),
            sem((slots, 2, ncols - 1)),
            sem((slots,)),
            sem((slots,)),
            sem((slots, 2)),
            sem((slots, 2)),
            sem((slots, ncols - 1, 2)),
            sem((slots, ncols - 1, 2)),
            sem((slots, ncols - 1)),
            sem((slots, ncols - 1)),
        ],
        compiler_params=pltpu.CompilerParams(vmem_limit_bytes=LIMIT, collective_id=0, has_side_effects=True),
        cost_estimate=pl.CostEstimate(
            flops=12 * slots * points * points * width, bytes_accessed=2 * tiles.size, transcendentals=0
        ),
        name="samples",
    )(weight, tiles, probe, cluster_perm)
    square = vmem((slots, width, width), f32)
    leaf_basis = pl.pallas_call(
        functools.partial(basis_kernel, points),
        out_shape=jax.ShapeDtypeStruct(samples.shape, f32),
        in_specs=[whole, whole],
        out_specs=whole,
        scratch_shapes=[square, square, square],
        compiler_params=pltpu.CompilerParams(vmem_limit_bytes=LIMIT),
        name="leaf_basis",
    )(samples, gram_sum)
    return (samples, leaf_basis)


def solution(mesh):
    placed = (
        P(None, "row", "col"),
        P(None, ("row", "col"), None),
        P(None, "row", None),
        P(None, "row", "col"),
    )
    return jax.shard_map(
        per_device,
        mesh=mesh,
        in_specs=placed,
        out_specs=(P(None, ("row", "col"), None), P(None, ("row", "col"), None)),
        check_vma=False,
    )
```

```python
import functools

import jax
import jax.numpy as jnp
from jax import lax
from jax.experimental import pallas as pl
from jax.experimental.pallas import tpu as pltpu
from jax.sharding import PartitionSpec as P

HIGHEST = lax.Precision.HIGHEST
LIMIT = 56 * 1024 * 1024
STEP = 256
NB = 64
AB_T = (((1,), (1,)), ((), ()))
AT_B = (((0,), (0,)), ((), ()))


def sort_rows(raw_ref, perm_ref, out_ref, slot):
    rows, width = out_ref.shape[1:]
    parts, per = raw_ref.shape[1:3]

    def block(index, carry):
        at = pl.multiple_of(index * STEP, STEP)
        order = jnp.broadcast_to(perm_ref[slot, :, pl.ds(at, STEP)], (128, STEP)).T
        total = jnp.zeros((STEP, width), jnp.float32)
        for part in range(parts):
            pieces = []
            for lane in range(part * per, part * per + per, 128):
                column = lax.broadcasted_iota(jnp.int32, (STEP, 128), 1) + lane
                pieces.append(jnp.where(order == column, 1.0, 0.0).astype(jnp.bfloat16))
            hot = jnp.concatenate(pieces, axis=1)
            total = total + jnp.dot(hot, raw_ref[slot, part], preferred_element_type=jnp.float32)
        out_ref[slot, pl.ds(at, STEP), :] = total.astype(out_ref.dtype)
        return carry

    lax.fori_loop(0, rows // STEP, block, 0)


def encode(value):
    top = jnp.max(jnp.abs(value), axis=1, keepdims=True)
    scale = jnp.where(top > 0.0, top, 1.0) * (1.0 / 32766.0)
    code = jnp.round(value * (1.0 / scale)).astype(jnp.int32).astype(jnp.int16)
    return code, scale


def decode(code, scale):
    value = code.astype(jnp.int32).astype(jnp.float32)
    scale = jnp.broadcast_to(scale, (128, scale.shape[1])).T
    return jnp.concatenate([value[:, lane:lane + 128] * scale for lane in range(0, value.shape[1], 128)], axis=1)


def as_lanes(scale):
    return jnp.broadcast_to(scale, (scale.shape[0], 128)).T[0:1]


def samples_kernel(
    nrows, n, weight_ref, tiles_ref, probe_ref, perm_ref, samples_ref, gram_ref,
    tile, raw, omega, far, back_code, back_scale, near_code, near_scale,
    combined, code, scale, got_code, got_scale, part_gram, got_gram,
    mid_code, mid_scale, last_code, last_scale,
    tile_sem, hop_send, hop_recv, far_send, far_recv, back_send, back_recv, own_send, own_recv, gram_send, gram_recv,
    mid_send, mid_recv, last_send, last_recv,
):
    slots, points, width = omega.shape
    per = points // n
    half = width // 2
    row, me = lax.axis_index("row"), lax.axis_index("col")
    before, after = lax.rem(row + nrows - me, nrows), lax.rem(row + me, nrows)
    from_wrap = jnp.where(row < me, 1, 0)
    to_wrap = jnp.where(row + me >= nrows, 1, 0)
    others = [lax.rem(me + o, n) for o in range(1, n)]
    mesh_id = pl.DeviceIdType.MESH
    in_row = lax.rem(me, 2) == 1
    evens = range(2, n, 2)

    def remote(src, dst, send, recv, where):
        return pltpu.make_async_remote_copy(
            src_ref=src, dst_ref=dst, send_sem=send, recv_sem=recv, device_id=where, device_id_type=mesh_id
        )

    def tile_copy(k):
        return pltpu.make_async_copy(tiles_ref.at[k], tile.at[k], tile_sem.at[k])

    def inside(at):
        return (at >= 0) & (at < n)

    def hop(k, side, s, block):
        step = 1 - 2 * side
        to = jnp.where(inside(me + step), me + step, me - step)
        src = probe_ref.at[k] if s == 0 else raw.at[k, block]
        return remote(src, raw.at[k, block], hop_send.at[k, side, s], hop_recv.at[k, side, s], {"col": to})

    def relay(k, s):
        for side in range(2):
            step = 1 - 2 * side
            block = me - s * step

            @pl.when(inside(block))
            def _():
                hop(k, side, s - 1, block).wait_recv()

            if s < n - 1:

                @pl.when(inside(block) & inside(me + step))
                def _():
                    hop(k, side, s, block).start()

    def far_copy(k):
        slot = lax.rem(k - from_wrap + slots, slots)
        return remote(omega.at[k], far.at[slot], far_send.at[k], far_recv.at[slot], {"row": before})

    def far_wait(slot):
        remote(omega.at[slot], far.at[slot], far_send.at[slot], far_recv.at[slot], {"row": before}).wait_recv()

    def back_copies(k, slot):
        return (
            remote(back_code.at[k], near_code.at[slot], back_send.at[k, 0], back_recv.at[slot, 0], {"row": after}),
            remote(back_scale.at[k], near_scale.at[slot], back_send.at[k, 1], back_recv.at[slot, 1], {"row": after}),
        )

    def mid_copies(k, e, o):
        to = others[o]
        lanes = pl.ds(pl.multiple_of(to * per, per), per)
        return (
            remote(back_code.at[k, lanes], mid_code.at[k, e], mid_send.at[k, o, 0], mid_recv.at[k, e, 0], {"col": to}),
            remote(
                back_scale.at[k, :, lanes], mid_scale.at[k, e], mid_send.at[k, o, 1], mid_recv.at[k, e, 1], {"col": to}
            ),
        )

    def last_copies(k, e, own):
        offset = evens[e]
        slot = lax.rem(k + jnp.where(row + offset >= nrows, 1, 0), slots)
        lanes = pl.ds(pl.multiple_of(me * per, per), per)
        sources = (back_code.at[k, lanes], back_scale.at[k, :, lanes]) if own else (mid_code.at[k, e], mid_scale.at[k, e])
        targets = (last_code.at[slot, e], last_scale.at[slot, e])
        to = {"row": lax.rem(row + offset, nrows)}
        return [
            remote(sources[i], targets[i], last_send.at[k, e, i], last_recv.at[slot, e, i], to) for i in range(2)
        ]

    def last_waits(slot, e):
        to = {"row": lax.rem(row + evens[e], nrows)}
        for i, buffer in enumerate((last_code, last_scale)):
            remote(
                mid_code.at[slot, e] if i == 0 else mid_scale.at[slot, e],
                buffer.at[slot, e], last_send.at[slot, e, i], last_recv.at[slot, e, i], to,
            ).wait_recv()

    def pass_on(k):
        for e, offset in enumerate(evens):

            @pl.when(me != offset)
            def _():
                for copy in mid_copies(k, e, 0):
                    copy.wait_recv()
                for copy in last_copies(k, e, False):
                    copy.start()

    def own_copies(k, o):
        to = others[o]
        return (
            remote(code.at[k, to], got_code.at[k, o], own_send.at[k, o, 0], own_recv.at[k, o, 0], {"col": to}),
            remote(scale.at[k, to], got_scale.at[k, o], own_send.at[k, o, 1], own_recv.at[k, o, 1], {"col": to}),
        )

    def gram_copy(k, o):
        return remote(part_gram.at[k], got_gram.at[k, o], gram_send.at[k, o], gram_recv.at[k, o], {"col": others[o]})

    def sort_and_send(k):
        sort_rows(raw, perm_ref, omega, k)

        @pl.when(me > 0)
        def _():
            far_copy(k).start()

    def backward(k):
        omega_t = omega[k].T

        def block(index, carry):
            at = pl.multiple_of(index * STEP, STEP)
            value = jnp.dot(omega_t, tile[k, :, pl.ds(at, STEP)], preferred_element_type=jnp.float32)
            coded, scales = encode(value.T * weight_ref[k])
            back_code[k, pl.ds(at, STEP), :] = coded
            back_scale[k, :, pl.ds(at, STEP)] = as_lanes(scales)
            return carry

        lax.fori_loop(0, points // STEP, block, 0)

        @pl.when(in_row)
        def _():
            for copy in back_copies(k, lax.rem(k + to_wrap, slots)):
                copy.start()

        for e, offset in enumerate(evens):

            @pl.when(me == offset)
            def _():
                for o in range(n - 1):
                    for copy in mid_copies(k, e, o):
                        copy.start()
                for copy in last_copies(k, e, True):
                    copy.start()

    def forward(k):

        @pl.when(me > 0)
        def _():
            far_wait(k)

        @pl.when(me == 0)
        def _():
            far[k] = omega[k]

        def block(index, carry):
            at = pl.multiple_of(index * per, per)
            value = jnp.dot(tile[k, pl.ds(at, per), :], far[k], preferred_element_type=jnp.float32)
            combined[k, index] = value * weight_ref[k]
            return carry

        lax.fori_loop(0, n, block, 0)

    def combine(k):

        @pl.when(in_row)
        def _():
            for copy in back_copies(k, k):
                copy.wait_recv()

        @pl.when(me == 0)
        def _():
            near_code[k] = back_code[k]
            near_scale[k] = back_scale[k]

        @pl.when(in_row | (me == 0))
        def _():

            def add(index, carry):
                at = pl.multiple_of(index * per, per)
                value = decode(near_code[k, pl.ds(at, per), :], near_scale[k, :, pl.ds(at, per)])
                combined[k, index] = combined[k, index] + value
                return carry

            lax.fori_loop(0, n, add, 0)

        def block(index, carry):
            coded, scales = encode(combined[k, index])
            code[k, index] = coded
            scale[k, index] = as_lanes(scales)
            return carry

        lax.fori_loop(0, n, block, 0)
        for o in range(n - 1):
            for copy in own_copies(k, o):
                copy.start()

    def collect(k):
        total = combined[k, me]
        for e in range(len(evens)):
            last_waits(k, e)
            total = total + decode(last_code[k, e], last_scale[k, e])
        for o in range(n - 1):
            for copy in own_copies(k, o):
                copy.wait_recv()
            total = total + decode(got_code[k, o], got_scale[k, o])
        samples_ref[k] = total
        total_t = total.T
        upper = jnp.dot(total_t[:half], total, precision=HIGHEST, preferred_element_type=jnp.float32)
        lower = jnp.dot(total_t[half:], total[:, half:], precision=HIGHEST, preferred_element_type=jnp.float32)
        part_gram[k, 0:half] = upper[:, :half]
        part_gram[k, half:2 * half] = upper[:, half:]
        part_gram[k, 2 * half:3 * half] = lower
        for o in range(n - 1):
            gram_copy(k, o).start()

    def gather_gram(k):
        total = part_gram[k]
        for o in range(n - 1):
            gram_copy(k, o).wait_recv()
            total = total + got_gram[k, o]
        gram_ref[k, 0:half, 0:half] = total[0:half]
        gram_ref[k, 0:half, half:] = total[half:2 * half]
        gram_ref[k, half:, 0:half] = total[half:2 * half].T
        gram_ref[k, half:, half:] = total[2 * half:]

    barrier = pltpu.get_barrier_semaphore()
    for to in others:
        pl.semaphore_signal(barrier, inc=1, device_id={"col": to}, device_id_type=mesh_id)

    for o in range(1, nrows):
        pl.semaphore_signal(barrier, inc=1, device_id={"row": lax.rem(row + o, nrows)}, device_id_type=mesh_id)
    pl.semaphore_wait(barrier, n + nrows - 2)
    for k in range(slots):
        for side in range(2):

            @pl.when(inside(me + 1 - 2 * side))
            def _():
                hop(k, side, 0, me).start()

    for k in range(slots):
        tile_copy(k).start()
        raw[k, me] = probe_ref[k]
    for s in range(1, n):
        relay(0, s)
    for k in range(slots):
        if k + 1 < slots:
            relay(k + 1, 1)
        sort_and_send(k)
        if k + 1 < slots:
            for s in range(2, n - 1):
                relay(k + 1, s)
        tile_copy(k).wait()
        backward(k)
        if k + 1 < slots:
            relay(k + 1, n - 1)
    for k in range(slots):
        pass_on(k)
        forward(k)
        combine(k)
    for k in range(slots):
        collect(k)
    for k in range(slots):
        gather_gram(k)

    for k in range(slots):
        for side in range(2):
            step = 1 - 2 * side
            for s in range(n - 1):

                @pl.when(inside(me - s * step) & inside(me + step))
                def _():
                    hop(k, side, s, me - s * step).wait_send()

        @pl.when(me > 0)
        def _():
            far_copy(k).wait_send()

        @pl.when(in_row)
        def _():
            for copy in back_copies(k, lax.rem(k + to_wrap, slots)):
                copy.wait_send()

        for e, offset in enumerate(evens):
            for copy in last_copies(k, e, False):
                copy.wait_send()

            @pl.when(me == offset)
            def _():
                for o in range(n - 1):
                    for copy in mid_copies(k, e, o):
                        copy.wait_send()

        for o in range(n - 1):
            for copy in own_copies(k, o):
                copy.wait_send()
            gram_copy(k, o).wait_send()


def reciprocal(value):
    guess = pl.reciprocal(value, approx=True)
    for _ in range(2):
        guess = guess * (2.0 - value * guess)
    return guess


def eliminate(squares):
    parts = NB // 8
    row_at = lax.broadcasted_iota(jnp.int32, (8, 128), 0)
    lane_at = lax.broadcasted_iota(jnp.int32, (8, 128), 1)
    work = [[square[8 * t:8 * t + 8, :] for t in range(parts)] for square in squares]
    unit = [[jnp.where(row_at + 8 * t == lane_at, 1.0, 0.0) for t in range(parts)] for _ in squares]
    for j in range(0, NB, 2):
        top, row = j // 8, j % 8
        for b in range(len(squares)):
            firsts = [jnp.broadcast_to(work[b][t][:, j:j + 1], (8, 128)) for t in range(top, parts)]
            seconds = [jnp.broadcast_to(work[b][t][:, j + 1:j + 2], (8, 128)) for t in range(top, parts)]
            head, cross, tail = firsts[0][row:row + 1], firsts[0][row + 1:row + 2], seconds[0][row + 1:row + 2]
            inverse = reciprocal(head * tail - cross * cross)
            ratio = cross * reciprocal(head)
            tail, cross, head = tail * inverse, cross * inverse, head * inverse
            pairs = [(array[b][top][row:row + 1], array[b][top][row + 1:row + 2]) for array in (work, unit)]
            for t in range(top, parts):
                one = firsts[t - top] * tail - seconds[t - top] * cross
                two = seconds[t - top] * head - firsts[t - top] * cross
                if t == top:
                    one = jnp.where(row_at > row + 1, one, jnp.where(row_at == row + 1, ratio, 0.0))
                    two = jnp.where(row_at > row + 1, two, 0.0)
                for array, (upper, lower) in zip((work, unit), pairs):
                    array[b][t] = array[b][t] - (one * upper + two * lower)
    inverses = []
    for b in range(len(squares)):
        scaled = []
        for t in range(parts):
            pivot = jnp.sum(jnp.where(row_at + 8 * t == lane_at, work[b][t], 0.0), axis=1, keepdims=True)
            scaled.append(unit[b][t] * lax.rsqrt(pivot))
        inverses.append(jnp.concatenate(scaled, axis=0)[:, :NB])
    return inverses


def invert_factors(gram_ref, unit_ref, inverse_ref):
    slots, size = gram_ref.shape[0], gram_ref.shape[1]
    row_at = lax.broadcasted_iota(jnp.int32, (size, size), 0)
    lane_at = lax.broadcasted_iota(jnp.int32, (size, size), 1)
    for k in range(slots):
        unit_ref[k] = jnp.where(row_at == lane_at, 1.0, 0.0)

    def panel(index, carry):
        inverses = eliminate([gram_ref[k, 0:NB, 0:128] for k in range(slots)])
        for k in range(slots):
            across = jnp.dot(inverses[k], gram_ref[k, 0:NB, :], precision=HIGHEST, preferred_element_type=jnp.float32)
            done = jnp.dot(inverses[k], unit_ref[k, 0:NB, :], precision=HIGHEST, preferred_element_type=jnp.float32)
            inverse_ref[k, pl.ds(pl.multiple_of(index * NB, NB), NB), :] = done
            across_t = across.T[NB:, :]
            less = jnp.dot(across_t, across, precision=HIGHEST, preferred_element_type=jnp.float32)
            gram_ref[k, 0:size - NB, :] = pltpu.roll(gram_ref[k, NB:, :] - less, size - NB, 1)
            less = jnp.dot(across_t, done, precision=HIGHEST, preferred_element_type=jnp.float32)
            unit_ref[k, 0:size - NB, :] = unit_ref[k, NB:, :] - less
        return carry

    lax.fori_loop(0, size // NB, panel, 0)


def basis_kernel(points, samples_ref, gram_ref, basis_ref, work_ref, unit_ref, inverse_ref):
    work_ref[...] = gram_ref[...] * (1.0 / points)
    invert_factors(work_ref, unit_ref, inverse_ref)
    for k in range(samples_ref.shape[0]):
        basis_ref[k] = lax.dot_general(
            samples_ref[k], inverse_ref[k], AB_T, precision=HIGHEST, preferred_element_type=jnp.float32
        )


def per_device(tiles, probe, cluster_perm, tile_keep):
    nrows = lax.axis_size("row")
    ncols = lax.axis_size("col")
    slots, points, _ = tiles.shape
    per, width = probe.shape[1:]
    half = width // 2
    evens = len(range(2, ncols, 2))
    whole = pl.BlockSpec(memory_space=pltpu.VMEM)
    weight = jnp.where(lax.axis_index("col") == 0, 0.5, tile_keep[:, 0, 0].astype(jnp.float32))
    vmem = pltpu.VMEM
    sem = pltpu.SemaphoreType.DMA
    bf16, f32, i16 = jnp.bfloat16, jnp.float32, jnp.int16
    samples, gram_sum = pl.pallas_call(
        functools.partial(samples_kernel, nrows, ncols),
        out_shape=(
            jax.ShapeDtypeStruct((slots, per, width), f32),
            jax.ShapeDtypeStruct((slots, width, width), f32),
        ),
        in_specs=[pl.BlockSpec(memory_space=pltpu.SMEM), pl.BlockSpec(memory_space=pl.ANY), whole, whole],
        out_specs=(whole, whole),
        scratch_shapes=[
            vmem((slots, points, points), bf16),
            vmem((slots, ncols, per, width), bf16),
            vmem((slots, points, width), bf16),
            vmem((slots, points, width), bf16),
            vmem((slots, points, width), i16),
            vmem((slots, 1, points), f32),
            vmem((slots, points, width), i16),
            vmem((slots, 1, points), f32),
            vmem((slots, ncols, per, width), f32),
            vmem((slots, ncols, per, width), i16),
            vmem((slots, ncols, 1, per), f32),
            vmem((slots, ncols - 1, per, width), i16),
            vmem((slots, ncols - 1, 1, per), f32),
            vmem((slots, 3 * half, half), f32),
            vmem((slots, ncols - 1, 3 * half, half), f32),
            vmem((slots, evens, per, width), i16),
            vmem((slots, evens, 1, per), f32),
            vmem((slots, evens, per, width), i16),
            vmem((slots, evens, 1, per), f32),
            sem((slots,)),
            sem((slots, 2, ncols - 1)),
            sem((slots, 2, ncols - 1)),
            sem((slots,)),
            sem((slots,)),
            sem((slots, 2)),
            sem((slots, 2)),
            sem((slots, ncols - 1, 2)),
            sem((slots, ncols - 1, 2)),
            sem((slots, ncols - 1)),
            sem((slots, ncols - 1)),
            sem((slots, ncols - 1, 2)),
            sem((slots, evens, 2)),
            sem((slots, evens, 2)),
            sem((slots, evens, 2)),
        ],
        compiler_params=pltpu.CompilerParams(vmem_limit_bytes=LIMIT, collective_id=0, has_side_effects=True),
        cost_estimate=pl.CostEstimate(
            flops=12 * slots * points * points * width, bytes_accessed=2 * tiles.size, transcendentals=0
        ),
        name="samples",
    )(weight, tiles, probe, cluster_perm)
    square = vmem((slots, width, width), f32)
    leaf_basis = pl.pallas_call(
        functools.partial(basis_kernel, points),
        out_shape=jax.ShapeDtypeStruct(samples.shape, f32),
        in_specs=[whole, whole],
        out_specs=whole,
        scratch_shapes=[square, square, square],
        compiler_params=pltpu.CompilerParams(vmem_limit_bytes=LIMIT),
        name="leaf_basis",
    )(samples, gram_sum)
    return (samples, leaf_basis)


def solution(mesh):
    placed = (
        P(None, "row", "col"),
        P(None, ("row", "col"), None),
        P(None, "row", None),
        P(None, "row", "col"),
    )
    return jax.shard_map(
        per_device,
        mesh=mesh,
        in_specs=placed,
        out_specs=(P(None, ("row", "col"), None), P(None, ("row", "col"), None)),
        check_vma=False,
    )
```

```python
import functools

import jax
import jax.numpy as jnp
from jax import lax
from jax.experimental import pallas as pl
from jax.experimental.pallas import tpu as pltpu
from jax.sharding import PartitionSpec as P

HIGHEST = lax.Precision.HIGHEST
LIMIT = 56 * 1024 * 1024
STEP = 256
NB = 64
AB_T = (((1,), (1,)), ((), ()))
AT_B = (((0,), (0,)), ((), ()))


def sort_rows(raw_ref, perm_ref, out_ref, slot):
    rows, width = out_ref.shape[1:]
    parts, per = raw_ref.shape[1:3]

    def block(index, carry):
        at = pl.multiple_of(index * STEP, STEP)
        order = jnp.broadcast_to(perm_ref[slot, :, pl.ds(at, STEP)], (128, STEP)).T
        total = jnp.zeros((STEP, width), jnp.float32)
        for part in range(parts):
            pieces = []
            for lane in range(part * per, part * per + per, 128):
                column = lax.broadcasted_iota(jnp.int32, (STEP, 128), 1) + lane
                pieces.append(jnp.where(order == column, 1.0, 0.0).astype(jnp.bfloat16))
            hot = jnp.concatenate(pieces, axis=1)
            total = total + jnp.dot(hot, raw_ref[slot, part], preferred_element_type=jnp.float32)
        out_ref[slot, pl.ds(at, STEP), :] = total.astype(out_ref.dtype)
        return carry

    lax.fori_loop(0, rows // STEP, block, 0)


def encode(value):
    top = jnp.max(jnp.abs(value), axis=1, keepdims=True)
    scale = jnp.where(top > 0.0, top, 1.0) * (1.0 / 32766.0)
    code = jnp.round(value * (1.0 / scale)).astype(jnp.int32).astype(jnp.int16)
    return code, scale


def decode(code, scale):
    value = code.astype(jnp.int32).astype(jnp.float32)
    scale = jnp.broadcast_to(scale, (128, scale.shape[1])).T
    return jnp.concatenate([value[:, lane:lane + 128] * scale for lane in range(0, value.shape[1], 128)], axis=1)


def as_lanes(scale):
    return jnp.broadcast_to(scale, (scale.shape[0], 128)).T[0:1]


def samples_kernel(
    nrows, n, weight_ref, tiles_ref, probe_ref, perm_ref, samples_ref, gram_ref,
    tile, raw, omega, far, back_code, back_scale, near_code, near_scale,
    combined, code, scale, got_code, got_scale, part_gram, up_gram, got_gram, all_gram,
    mid_code, mid_scale, last_code, last_scale,
    tile_sem, hop_send, hop_recv, far_send, far_recv, back_send, back_recv, own_send, own_recv, gram_send, gram_recv,
    mid_send, mid_recv, last_send, last_recv,
):
    slots, points, width = omega.shape
    per = points // n
    half = width // 2
    row, me = lax.axis_index("row"), lax.axis_index("col")
    before, after = lax.rem(row + nrows - me, nrows), lax.rem(row + me, nrows)
    from_wrap = jnp.where(row < me, 1, 0)
    to_wrap = jnp.where(row + me >= nrows, 1, 0)
    others = [lax.rem(me + o, n) for o in range(1, n)]
    mesh_id = pl.DeviceIdType.MESH
    in_row = lax.rem(me, 2) == 1
    evens = range(2, n, 2)

    def remote(src, dst, send, recv, where):
        return pltpu.make_async_remote_copy(
            src_ref=src, dst_ref=dst, send_sem=send, recv_sem=recv, device_id=where, device_id_type=mesh_id
        )

    def tile_copy(k):
        return pltpu.make_async_copy(tiles_ref.at[k], tile.at[k], tile_sem.at[k])

    def inside(at):
        return (at >= 0) & (at < n)

    def hop(k, side, s, block):
        step = 1 - 2 * side
        to = jnp.where(inside(me + step), me + step, me - step)
        src = probe_ref.at[k] if s == 0 else raw.at[k, block]
        return remote(src, raw.at[k, block], hop_send.at[k, side, s], hop_recv.at[k, side, s], {"col": to})

    def relay(k, s):
        for side in range(2):
            step = 1 - 2 * side
            block = me - s * step

            @pl.when(inside(block))
            def _():
                hop(k, side, s - 1, block).wait_recv()

            if s < n - 1:

                @pl.when(inside(block) & inside(me + step))
                def _():
                    hop(k, side, s, block).start()

    def far_copy(k):
        slot = lax.rem(k - from_wrap + slots, slots)
        return remote(omega.at[k], far.at[slot], far_send.at[k], far_recv.at[slot], {"row": before})

    def far_wait(slot):
        remote(omega.at[slot], far.at[slot], far_send.at[slot], far_recv.at[slot], {"row": before}).wait_recv()

    def back_copies(k, slot):
        return (
            remote(back_code.at[k], near_code.at[slot], back_send.at[k, 0], back_recv.at[slot, 0], {"row": after}),
            remote(back_scale.at[k], near_scale.at[slot], back_send.at[k, 1], back_recv.at[slot, 1], {"row": after}),
        )

    def mid_copies(k, e, o):
        to = others[o]
        lanes = pl.ds(pl.multiple_of(to * per, per), per)
        return (
            remote(back_code.at[k, lanes], mid_code.at[k, e], mid_send.at[k, o, 0], mid_recv.at[k, e, 0], {"col": to}),
            remote(
                back_scale.at[k, :, lanes], mid_scale.at[k, e], mid_send.at[k, o, 1], mid_recv.at[k, e, 1], {"col": to}
            ),
        )

    def last_copies(k, e, own):
        offset = evens[e]
        slot = lax.rem(k + jnp.where(row + offset >= nrows, 1, 0), slots)
        lanes = pl.ds(pl.multiple_of(me * per, per), per)
        sources = (back_code.at[k, lanes], back_scale.at[k, :, lanes]) if own else (mid_code.at[k, e], mid_scale.at[k, e])
        targets = (last_code.at[slot, e], last_scale.at[slot, e])
        to = {"row": lax.rem(row + offset, nrows)}
        return [
            remote(sources[i], targets[i], last_send.at[k, e, i], last_recv.at[slot, e, i], to) for i in range(2)
        ]

    def last_waits(slot, e):
        to = {"row": lax.rem(row + evens[e], nrows)}
        for i, buffer in enumerate((last_code, last_scale)):
            remote(
                mid_code.at[slot, e] if i == 0 else mid_scale.at[slot, e],
                buffer.at[slot, e], last_send.at[slot, e, i], last_recv.at[slot, e, i], to,
            ).wait_recv()

    def pass_on(k):
        for e, offset in enumerate(evens):

            @pl.when(me != offset)
            def _():
                for copy in mid_copies(k, e, 0):
                    copy.wait_recv()
                for copy in last_copies(k, e, False):
                    copy.start()

    def own_copies(k, side, block):
        step = 1 - 2 * side
        to = {"col": jnp.where(inside(me + step), me + step, me - step)}
        return (
            remote(code.at[k, block], got_code.at[k, side, block], own_send.at[k, block, 0], own_recv.at[k, side, block, 0], to),
            remote(scale.at[k, block], got_scale.at[k, side, block], own_send.at[k, block, 1], own_recv.at[k, side, block, 1], to),
        )

    middle = n // 2
    inward = jnp.where(me < middle, 1, -1)
    is_middle = (me == middle - 1) | (me == middle)
    is_end = (me == 0) | (me == n - 1)
    inner = {"col": me + inward}
    outer = {"col": jnp.where(is_end, me + inward, me - inward)}

    def gram_up(k):
        return remote(part_gram.at[k], up_gram.at[k], gram_send.at[k, 0], gram_recv.at[k, 0], inner)

    def gram_across(k):
        return remote(part_gram.at[k], got_gram.at[k], gram_send.at[k, 0], gram_recv.at[k, 1], inner)

    def gram_down(k):
        return remote(all_gram.at[k], got_gram.at[k], gram_send.at[k, 1], gram_recv.at[k, 1], outer)

    def sort_and_send(k):
        sort_rows(raw, perm_ref, omega, k)

        @pl.when(me > 0)
        def _():
            far_copy(k).start()

    def backward(k):
        omega_t = omega[k].T

        def block(index, carry):
            at = pl.multiple_of(index * STEP, STEP)
            value = jnp.dot(omega_t, tile[k, :, pl.ds(at, STEP)], preferred_element_type=jnp.float32)
            coded, scales = encode(value.T * weight_ref[k])
            back_code[k, pl.ds(at, STEP), :] = coded
            back_scale[k, :, pl.ds(at, STEP)] = as_lanes(scales)
            return carry

        lax.fori_loop(0, points // STEP, block, 0)

        @pl.when(in_row)
        def _():
            for copy in back_copies(k, lax.rem(k + to_wrap, slots)):
                copy.start()

        for e, offset in enumerate(evens):

            @pl.when(me == offset)
            def _():
                for o in range(n - 1):
                    for copy in mid_copies(k, e, o):
                        copy.start()
                for copy in last_copies(k, e, True):
                    copy.start()

    def forward(k):

        @pl.when(me > 0)
        def _():
            far_wait(k)

        @pl.when(me == 0)
        def _():
            far[k] = omega[k]

        def block(index, carry):
            at = pl.multiple_of(index * per, per)
            value = jnp.dot(tile[k, pl.ds(at, per), :], far[k], preferred_element_type=jnp.float32)
            combined[k, index] = value * weight_ref[k]
            return carry

        lax.fori_loop(0, n, block, 0)

    def combine(k):

        @pl.when(in_row)
        def _():
            for copy in back_copies(k, k):
                copy.wait_recv()

        @pl.when(me == 0)
        def _():
            near_code[k] = back_code[k]
            near_scale[k] = back_scale[k]

        @pl.when(in_row | (me == 0))
        def _():

            def add(index, carry):
                at = pl.multiple_of(index * per, per)
                value = decode(near_code[k, pl.ds(at, per), :], near_scale[k, :, pl.ds(at, per)])
                combined[k, index] = combined[k, index] + value
                return carry

            lax.fori_loop(0, n, add, 0)

        for i in range(n - 1):
            for side, block in ((0, n - 1 - i), (1, i)):
                sends = me < block if side == 0 else me > block
                first = me == 0 if side == 0 else me == n - 1

                @pl.when(sends & jnp.logical_not(first))
                def _():
                    for copy in own_copies(k, side, block):
                        copy.wait_recv()
                    combined[k, block] = combined[k, block] + decode(got_code[k, side, block], got_scale[k, side, block])

                @pl.when(sends)
                def _():
                    coded, scales = encode(combined[k, block])
                    code[k, block] = coded
                    scale[k, block] = as_lanes(scales)
                    for copy in own_copies(k, side, block):
                        copy.start()

    def collect(k):
        samples_ref[k] = combined[k, me]
        for e in range(len(evens)):
            last_waits(k, e)
            samples_ref[k] = samples_ref[k] + decode(last_code[k, e], last_scale[k, e])
        for side in range(2):

            @pl.when(inside(me - 1 + 2 * side))
            def _():
                for copy in own_copies(k, side, me):
                    copy.wait_recv()
                samples_ref[k] = samples_ref[k] + decode(got_code[k, side, me], got_scale[k, side, me])

        total = samples_ref[k]
        total_t = total.T
        upper = jnp.dot(total_t[:half], total, precision=HIGHEST, preferred_element_type=jnp.float32)
        lower = jnp.dot(total_t[half:], total[:, half:], precision=HIGHEST, preferred_element_type=jnp.float32)
        part_gram[k, 0:half] = upper[:, :half]
        part_gram[k, half:2 * half] = upper[:, half:]
        part_gram[k, 2 * half:3 * half] = lower

    def sum_inward(k):

        @pl.when(jnp.logical_not(is_end))
        def _():
            gram_up(k).wait_recv()
            part_gram[k] = part_gram[k] + up_gram[k]

        @pl.when(is_middle)
        def _():
            gram_across(k).start()

        @pl.when(jnp.logical_not(is_middle))
        def _():
            gram_up(k).start()

    def send_outward(k):
        gram_across(k).wait_recv()

        @pl.when(is_middle)
        def _():
            all_gram[k] = part_gram[k] + got_gram[k]

        @pl.when(jnp.logical_not(is_middle))
        def _():
            all_gram[k] = got_gram[k]

        @pl.when(jnp.logical_not(is_end))
        def _():
            gram_down(k).start()

        total = all_gram[k]
        gram_ref[k, 0:half, 0:half] = total[0:half]
        gram_ref[k, 0:half, half:] = total[half:2 * half]
        gram_ref[k, half:, 0:half] = total[half:2 * half].T
        gram_ref[k, half:, half:] = total[2 * half:]

    barrier = pltpu.get_barrier_semaphore()
    for to in others:
        pl.semaphore_signal(barrier, inc=1, device_id={"col": to}, device_id_type=mesh_id)

    for o in range(1, nrows):
        pl.semaphore_signal(barrier, inc=1, device_id={"row": lax.rem(row + o, nrows)}, device_id_type=mesh_id)
    pl.semaphore_wait(barrier, n + nrows - 2)
    for k in range(slots):
        for side in range(2):

            @pl.when(inside(me + 1 - 2 * side))
            def _():
                hop(k, side, 0, me).start()

    for k in range(slots):
        tile_copy(k).start()
        raw[k, me] = probe_ref[k]
    for s in range(1, n):
        relay(0, s)
    for k in range(slots):
        if k + 1 < slots:
            relay(k + 1, 1)
        sort_and_send(k)
        if k + 1 < slots:
            for s in range(2, n - 1):
                relay(k + 1, s)
        tile_copy(k).wait()
        backward(k)
        if k + 1 < slots:
            relay(k + 1, n - 1)
    pass_on(0)
    for k in range(slots):
        forward(k)
        if k + 1 < slots:
            pass_on(k + 1)
        combine(k)
    for k in range(slots):
        collect(k)
        sum_inward(k)
        if k > 0:
            send_outward(k - 1)
    send_outward(slots - 1)

    for k in range(slots):
        for side in range(2):
            step = 1 - 2 * side
            for s in range(n - 1):

                @pl.when(inside(me - s * step) & inside(me + step))
                def _():
                    hop(k, side, s, me - s * step).wait_send()

        @pl.when(me > 0)
        def _():
            far_copy(k).wait_send()

        @pl.when(in_row)
        def _():
            for copy in back_copies(k, lax.rem(k + to_wrap, slots)):
                copy.wait_send()

        for e, offset in enumerate(evens):
            for copy in last_copies(k, e, False):
                copy.wait_send()

            @pl.when(me == offset)
            def _():
                for o in range(n - 1):
                    for copy in mid_copies(k, e, o):
                        copy.wait_send()

        for side in range(2):
            for block in range(n):

                @pl.when(me < block if side == 0 else me > block)
                def _():
                    for copy in own_copies(k, side, block):
                        copy.wait_send()

        gram_across(k).wait_send()

        @pl.when(jnp.logical_not(is_end))
        def _():
            gram_down(k).wait_send()


def reciprocal(value):
    guess = pl.reciprocal(value, approx=True)
    for _ in range(2):
        guess = guess * (2.0 - value * guess)
    return guess


def eliminate(squares):
    parts = NB // 8
    row_at = lax.broadcasted_iota(jnp.int32, (8, 128), 0)
    lane_at = lax.broadcasted_iota(jnp.int32, (8, 128), 1)
    work = [[square[8 * t:8 * t + 8, :] for t in range(parts)] for square in squares]
    unit = [[jnp.where(row_at + 8 * t == lane_at, 1.0, 0.0) for t in range(parts)] for _ in squares]
    for j in range(0, NB, 2):
        top, row = j // 8, j % 8
        for b in range(len(squares)):
            firsts = [jnp.broadcast_to(work[b][t][:, j:j + 1], (8, 128)) for t in range(top, parts)]
            seconds = [jnp.broadcast_to(work[b][t][:, j + 1:j + 2], (8, 128)) for t in range(top, parts)]
            head, cross, tail = firsts[0][row:row + 1], firsts[0][row + 1:row + 2], seconds[0][row + 1:row + 2]
            inverse = reciprocal(head * tail - cross * cross)
            ratio = cross * reciprocal(head)
            tail, cross, head = tail * inverse, cross * inverse, head * inverse
            pairs = [(array[b][top][row:row + 1], array[b][top][row + 1:row + 2]) for array in (work, unit)]
            for t in range(top, parts):
                one = firsts[t - top] * tail - seconds[t - top] * cross
                two = seconds[t - top] * head - firsts[t - top] * cross
                if t == top:
                    one = jnp.where(row_at > row + 1, one, jnp.where(row_at == row + 1, ratio, 0.0))
                    two = jnp.where(row_at > row + 1, two, 0.0)
                for array, (upper, lower) in zip((work, unit), pairs):
                    array[b][t] = array[b][t] - (one * upper + two * lower)
    inverses = []
    for b in range(len(squares)):
        scaled = []
        for t in range(parts):
            pivot = jnp.sum(jnp.where(row_at + 8 * t == lane_at, work[b][t], 0.0), axis=1, keepdims=True)
            scaled.append(unit[b][t] * lax.rsqrt(pivot))
        inverses.append(jnp.concatenate(scaled, axis=0)[:, :NB])
    return inverses


def invert_factors(gram_ref, unit_ref, inverse_ref):
    slots, size = gram_ref.shape[0], gram_ref.shape[1]
    row_at = lax.broadcasted_iota(jnp.int32, (size, size), 0)
    lane_at = lax.broadcasted_iota(jnp.int32, (size, size), 1)
    for k in range(slots):
        unit_ref[k] = jnp.where(row_at == lane_at, 1.0, 0.0)

    def panel(index, carry):
        inverses = eliminate([gram_ref[k, 0:NB, 0:128] for k in range(slots)])
        for k in range(slots):
            across = jnp.dot(inverses[k], gram_ref[k, 0:NB, :], precision=HIGHEST, preferred_element_type=jnp.float32)
            done = jnp.dot(inverses[k], unit_ref[k, 0:NB, :], precision=HIGHEST, preferred_element_type=jnp.float32)
            inverse_ref[k, pl.ds(pl.multiple_of(index * NB, NB), NB), :] = done
            across_t = across.T[NB:, :]
            less = jnp.dot(across_t, across, precision=HIGHEST, preferred_element_type=jnp.float32)
            gram_ref[k, 0:size - NB, :] = pltpu.roll(gram_ref[k, NB:, :] - less, size - NB, 1)
            less = jnp.dot(across_t, done, precision=HIGHEST, preferred_element_type=jnp.float32)
            unit_ref[k, 0:size - NB, :] = unit_ref[k, NB:, :] - less
        return carry

    lax.fori_loop(0, size // NB, panel, 0)


def basis_kernel(points, samples_ref, gram_ref, basis_ref, work_ref, unit_ref, inverse_ref):
    work_ref[...] = gram_ref[...] * (1.0 / points)
    invert_factors(work_ref, unit_ref, inverse_ref)
    for k in range(samples_ref.shape[0]):
        basis_ref[k] = lax.dot_general(
            samples_ref[k], inverse_ref[k], AB_T, precision=HIGHEST, preferred_element_type=jnp.float32
        )


def per_device(tiles, probe, cluster_perm, tile_keep):
    nrows = lax.axis_size("row")
    ncols = lax.axis_size("col")
    slots, points, _ = tiles.shape
    per, width = probe.shape[1:]
    half = width // 2
    evens = len(range(2, ncols, 2))
    whole = pl.BlockSpec(memory_space=pltpu.VMEM)
    weight = jnp.where(lax.axis_index("col") == 0, 0.5, tile_keep[:, 0, 0].astype(jnp.float32))
    vmem = pltpu.VMEM
    sem = pltpu.SemaphoreType.DMA
    bf16, f32, i16 = jnp.bfloat16, jnp.float32, jnp.int16
    samples, gram_sum = pl.pallas_call(
        functools.partial(samples_kernel, nrows, ncols),
        out_shape=(
            jax.ShapeDtypeStruct((slots, per, width), f32),
            jax.ShapeDtypeStruct((slots, width, width), f32),
        ),
        in_specs=[pl.BlockSpec(memory_space=pltpu.SMEM), pl.BlockSpec(memory_space=pl.ANY), whole, whole],
        out_specs=(whole, whole),
        scratch_shapes=[
            vmem((slots, points, points), bf16),
            vmem((slots, ncols, per, width), bf16),
            vmem((slots, points, width), bf16),
            vmem((slots, points, width), bf16),
            vmem((slots, points, width), i16),
            vmem((slots, 1, points), f32),
            vmem((slots, points, width), i16),
            vmem((slots, 1, points), f32),
            vmem((slots, ncols, per, width), f32),
            vmem((slots, ncols, per, width), i16),
            vmem((slots, ncols, 1, per), f32),
            vmem((slots, 2, ncols, per, width), i16),
            vmem((slots, 2, ncols, 1, per), f32),
            vmem((slots, 3 * half, half), f32),
            vmem((slots, 3 * half, half), f32),
            vmem((slots, 3 * half, half), f32),
            vmem((slots, 3 * half, half), f32),
            vmem((slots, evens, per, width), i16),
            vmem((slots, evens, 1, per), f32),
            vmem((slots, evens, per, width), i16),
            vmem((slots, evens, 1, per), f32),
            sem((slots,)),
            sem((slots, 2, ncols - 1)),
            sem((slots, 2, ncols - 1)),
            sem((slots,)),
            sem((slots,)),
            sem((slots, 2)),
            sem((slots, 2)),
            sem((slots, ncols, 2)),
            sem((slots, 2, ncols, 2)),
            sem((slots, 2)),
            sem((slots, 2)),
            sem((slots, ncols - 1, 2)),
            sem((slots, evens, 2)),
            sem((slots, evens, 2)),
            sem((slots, evens, 2)),
        ],
        compiler_params=pltpu.CompilerParams(vmem_limit_bytes=LIMIT, collective_id=0, has_side_effects=True),
        cost_estimate=pl.CostEstimate(
            flops=12 * slots * points * points * width, bytes_accessed=2 * tiles.size, transcendentals=0
        ),
        name="samples",
    )(weight, tiles, probe, cluster_perm)
    square = vmem((slots, width, width), f32)
    leaf_basis = pl.pallas_call(
        functools.partial(basis_kernel, points),
        out_shape=jax.ShapeDtypeStruct(samples.shape, f32),
        in_specs=[whole, whole],
        out_specs=whole,
        scratch_shapes=[square, square, square],
        compiler_params=pltpu.CompilerParams(vmem_limit_bytes=LIMIT),
        name="leaf_basis",
    )(samples, gram_sum)
    return (samples, leaf_basis)


def solution(mesh):
    placed = (
        P(None, "row", "col"),
        P(None, ("row", "col"), None),
        P(None, "row", None),
        P(None, "row", "col"),
    )
    return jax.shard_map(
        per_device,
        mesh=mesh,
        in_specs=placed,
        out_specs=(P(None, ("row", "col"), None), P(None, ("row", "col"), None)),
        check_vma=False,
    )
```

```python
import functools

import jax
import jax.numpy as jnp
from jax import lax
from jax.experimental import pallas as pl
from jax.experimental.pallas import tpu as pltpu
from jax.sharding import PartitionSpec as P

HIGHEST = lax.Precision.HIGHEST
LIMIT = 56 * 1024 * 1024
STEP = 256
NB = 64
AB_T = (((1,), (1,)), ((), ()))
AT_B = (((0,), (0,)), ((), ()))


def sort_rows(raw_ref, perm_ref, out_ref, slot):
    rows, width = out_ref.shape[1:]
    parts, per = raw_ref.shape[1:3]

    def block(index, carry):
        at = pl.multiple_of(index * STEP, STEP)
        order = jnp.broadcast_to(perm_ref[slot, :, pl.ds(at, STEP)], (128, STEP)).T
        total = jnp.zeros((STEP, width), jnp.float32)
        for part in range(parts):
            pieces = []
            for lane in range(part * per, part * per + per, 128):
                column = lax.broadcasted_iota(jnp.int32, (STEP, 128), 1) + lane
                pieces.append(jnp.where(order == column, 1.0, 0.0).astype(jnp.bfloat16))
            hot = jnp.concatenate(pieces, axis=1)
            total = total + jnp.dot(hot, raw_ref[slot, part], preferred_element_type=jnp.float32)
        out_ref[slot, pl.ds(at, STEP), :] = total.astype(out_ref.dtype)
        return carry

    lax.fori_loop(0, rows // STEP, block, 0)


def encode(value):
    top = jnp.max(jnp.abs(value), axis=1, keepdims=True)
    scale = jnp.where(top > 0.0, top, 1.0) * (1.0 / 32766.0)
    code = jnp.round(value * (1.0 / scale)).astype(jnp.int32).astype(jnp.int16)
    return code, scale


def decode(code, scale):
    value = code.astype(jnp.int32).astype(jnp.float32)
    scale = jnp.broadcast_to(scale, (128, scale.shape[1])).T
    return jnp.concatenate([value[:, lane:lane + 128] * scale for lane in range(0, value.shape[1], 128)], axis=1)


def as_lanes(scale):
    return jnp.broadcast_to(scale, (scale.shape[0], 128)).T[0:1]


def samples_kernel(
    nrows, n, weight_ref, tiles_ref, probe_ref, perm_ref, samples_ref, gram_ref,
    tile, raw, omega, far, back_code, back_scale, near_code, near_scale,
    combined, code, scale, got_code, got_scale, part_gram, up_gram, got_gram, all_gram,
    mid_code, mid_scale, last_code, last_scale,
    tile_sem, hop_send, hop_recv, far_send, far_recv, back_send, back_recv, own_send, own_recv, gram_send, gram_recv,
    mid_send, mid_recv, last_send, last_recv,
):
    slots, points, width = omega.shape
    per = points // n
    half = width // 2
    row, me = lax.axis_index("row"), lax.axis_index("col")
    before, after = lax.rem(row + nrows - me, nrows), lax.rem(row + me, nrows)
    from_wrap = jnp.where(row < me, 1, 0)
    to_wrap = jnp.where(row + me >= nrows, 1, 0)
    others = [lax.rem(me + o, n) for o in range(1, n)]
    mesh_id = pl.DeviceIdType.MESH
    in_row = me == 1
    relayed = range(2, n)

    def remote(src, dst, send, recv, where):
        return pltpu.make_async_remote_copy(
            src_ref=src, dst_ref=dst, send_sem=send, recv_sem=recv, device_id=where, device_id_type=mesh_id
        )

    def tile_copy(k):
        return pltpu.make_async_copy(tiles_ref.at[k], tile.at[k], tile_sem.at[k])

    def inside(at):
        return (at >= 0) & (at < n)

    def hop(k, side, s, block):
        step = 1 - 2 * side
        to = jnp.where(inside(me + step), me + step, me - step)
        src = probe_ref.at[k] if s == 0 else raw.at[k, block]
        return remote(src, raw.at[k, block], hop_send.at[k, side, s], hop_recv.at[k, side, s], {"col": to})

    def relay(k, s):
        for side in range(2):
            step = 1 - 2 * side
            block = me - s * step

            @pl.when(inside(block))
            def _():
                hop(k, side, s - 1, block).wait_recv()

            if s < n - 1:

                @pl.when(inside(block) & inside(me + step))
                def _():
                    hop(k, side, s, block).start()

    def far_copy(k):
        slot = lax.rem(k - from_wrap + slots, slots)
        return remote(omega.at[k], far.at[slot], far_send.at[k], far_recv.at[slot], {"row": before})

    def far_wait(slot):
        remote(omega.at[slot], far.at[slot], far_send.at[slot], far_recv.at[slot], {"row": before}).wait_recv()

    def back_copies(k, slot):
        return (
            remote(back_code.at[k], near_code.at[slot], back_send.at[k, 0], back_recv.at[slot, 0], {"row": after}),
            remote(back_scale.at[k], near_scale.at[slot], back_send.at[k, 1], back_recv.at[slot, 1], {"row": after}),
        )

    def mid_copies(k, e, o):
        to = others[o]
        lanes = pl.ds(pl.multiple_of(to * per, per), per)
        return (
            remote(back_code.at[k, lanes], mid_code.at[k, e], mid_send.at[k, o, 0], mid_recv.at[k, e, 0], {"col": to}),
            remote(
                back_scale.at[k, :, lanes], mid_scale.at[k, e], mid_send.at[k, o, 1], mid_recv.at[k, e, 1], {"col": to}
            ),
        )

    def last_copies(k, e, own):
        offset = relayed[e]
        slot = lax.rem(k + jnp.where(row + offset >= nrows, 1, 0), slots)
        lanes = pl.ds(pl.multiple_of(me * per, per), per)
        sources = (back_code.at[k, lanes], back_scale.at[k, :, lanes]) if own else (mid_code.at[k, e], mid_scale.at[k, e])
        targets = (last_code.at[slot, e], last_scale.at[slot, e])
        to = {"row": lax.rem(row + offset, nrows)}
        return [
            remote(sources[i], targets[i], last_send.at[k, e, i], last_recv.at[slot, e, i], to) for i in range(2)
        ]

    def last_waits(slot, e):
        to = {"row": lax.rem(row + relayed[e], nrows)}
        for i, buffer in enumerate((last_code, last_scale)):
            remote(
                mid_code.at[slot, e] if i == 0 else mid_scale.at[slot, e],
                buffer.at[slot, e], last_send.at[slot, e, i], last_recv.at[slot, e, i], to,
            ).wait_recv()

    def pass_on(k):
        for e, offset in enumerate(relayed):

            @pl.when(me != offset)
            def _():
                for copy in mid_copies(k, e, 0):
                    copy.wait_recv()
                for copy in last_copies(k, e, False):
                    copy.start()

    def own_copies(k, side, block):
        step = 1 - 2 * side
        to = {"col": jnp.where(inside(me + step), me + step, me - step)}
        return (
            remote(code.at[k, block], got_code.at[k, side, block], own_send.at[k, block, 0], own_recv.at[k, side, block, 0], to),
            remote(scale.at[k, block], got_scale.at[k, side, block], own_send.at[k, block, 1], own_recv.at[k, side, block, 1], to),
        )

    middle = n // 2
    inward = jnp.where(me < middle, 1, -1)
    is_middle = (me == middle - 1) | (me == middle)
    is_end = (me == 0) | (me == n - 1)
    inner = {"col": me + inward}
    outer = {"col": jnp.where(is_end, me + inward, me - inward)}

    def gram_up(k):
        return remote(part_gram.at[k], up_gram.at[k], gram_send.at[k, 0], gram_recv.at[k, 0], inner)

    def gram_across(k):
        return remote(part_gram.at[k], got_gram.at[k], gram_send.at[k, 0], gram_recv.at[k, 1], inner)

    def gram_down(k):
        return remote(all_gram.at[k], got_gram.at[k], gram_send.at[k, 1], gram_recv.at[k, 1], outer)

    def sort_and_send(k):
        sort_rows(raw, perm_ref, omega, k)

        @pl.when(me > 0)
        def _():
            far_copy(k).start()

    def backward(k):
        omega_t = omega[k].T

        def block(index, carry):
            at = pl.multiple_of(index * STEP, STEP)
            value = jnp.dot(omega_t, tile[k, :, pl.ds(at, STEP)], preferred_element_type=jnp.float32)
            coded, scales = encode(value.T * weight_ref[k])
            back_code[k, pl.ds(at, STEP), :] = coded
            back_scale[k, :, pl.ds(at, STEP)] = as_lanes(scales)
            return carry

        lax.fori_loop(0, points // STEP, block, 0)

        @pl.when(in_row)
        def _():
            for copy in back_copies(k, lax.rem(k + to_wrap, slots)):
                copy.start()

        for e, offset in enumerate(relayed):

            @pl.when(me == offset)
            def _():
                for o in range(n - 1):
                    for copy in mid_copies(k, e, o):
                        copy.start()
                for copy in last_copies(k, e, True):
                    copy.start()

    def forward(k):

        @pl.when(me > 0)
        def _():
            far_wait(k)

        @pl.when(me == 0)
        def _():
            far[k] = omega[k]

        def block(index, carry):
            at = pl.multiple_of(index * per, per)
            value = jnp.dot(tile[k, pl.ds(at, per), :], far[k], preferred_element_type=jnp.float32)
            combined[k, index] = value * weight_ref[k]
            return carry

        lax.fori_loop(0, n, block, 0)

    def combine(k):

        @pl.when(in_row)
        def _():
            for copy in back_copies(k, k):
                copy.wait_recv()

        @pl.when(me == 0)
        def _():
            near_code[k] = back_code[k]
            near_scale[k] = back_scale[k]

        @pl.when(in_row | (me == 0))
        def _():

            def add(index, carry):
                at = pl.multiple_of(index * per, per)
                value = decode(near_code[k, pl.ds(at, per), :], near_scale[k, :, pl.ds(at, per)])
                combined[k, index] = combined[k, index] + value
                return carry

            lax.fori_loop(0, n, add, 0)

        for i in range(n - 1):
            for side, block in ((0, n - 1 - i), (1, i)):
                sends = me < block if side == 0 else me > block
                first = me == 0 if side == 0 else me == n - 1

                @pl.when(sends & jnp.logical_not(first))
                def _():
                    for copy in own_copies(k, side, block):
                        copy.wait_recv()
                    combined[k, block] = combined[k, block] + decode(got_code[k, side, block], got_scale[k, side, block])

                @pl.when(sends)
                def _():
                    coded, scales = encode(combined[k, block])
                    code[k, block] = coded
                    scale[k, block] = as_lanes(scales)
                    for copy in own_copies(k, side, block):
                        copy.start()

    def collect(k):
        samples_ref[k] = combined[k, me]
        for e in range(len(relayed)):
            last_waits(k, e)
            samples_ref[k] = samples_ref[k] + decode(last_code[k, e], last_scale[k, e])
        for side in range(2):

            @pl.when(inside(me - 1 + 2 * side))
            def _():
                for copy in own_copies(k, side, me):
                    copy.wait_recv()
                samples_ref[k] = samples_ref[k] + decode(got_code[k, side, me], got_scale[k, side, me])

        total = samples_ref[k]
        total_t = total.T
        upper = jnp.dot(total_t[:half], total, precision=HIGHEST, preferred_element_type=jnp.float32)
        lower = jnp.dot(total_t[half:], total[:, half:], precision=HIGHEST, preferred_element_type=jnp.float32)
        part_gram[k, 0:half] = upper[:, :half]
        part_gram[k, half:2 * half] = upper[:, half:]
        part_gram[k, 2 * half:3 * half] = lower

    def sum_inward(k):

        @pl.when(jnp.logical_not(is_end))
        def _():
            gram_up(k).wait_recv()
            part_gram[k] = part_gram[k] + up_gram[k]

        @pl.when(is_middle)
        def _():
            gram_across(k).start()

        @pl.when(jnp.logical_not(is_middle))
        def _():
            gram_up(k).start()

    def send_outward(k):
        gram_across(k).wait_recv()

        @pl.when(is_middle)
        def _():
            all_gram[k] = part_gram[k] + got_gram[k]

        @pl.when(jnp.logical_not(is_middle))
        def _():
            all_gram[k] = got_gram[k]

        @pl.when(jnp.logical_not(is_end))
        def _():
            gram_down(k).start()

        total = all_gram[k]
        gram_ref[k, 0:half, 0:half] = total[0:half]
        gram_ref[k, 0:half, half:] = total[half:2 * half]
        gram_ref[k, half:, 0:half] = total[half:2 * half].T
        gram_ref[k, half:, half:] = total[2 * half:]

    barrier = pltpu.get_barrier_semaphore()
    for to in others:
        pl.semaphore_signal(barrier, inc=1, device_id={"col": to}, device_id_type=mesh_id)

    for o in range(1, nrows):
        pl.semaphore_signal(barrier, inc=1, device_id={"row": lax.rem(row + o, nrows)}, device_id_type=mesh_id)
    pl.semaphore_wait(barrier, n + nrows - 2)
    for k in range(slots):
        for side in range(2):

            @pl.when(inside(me + 1 - 2 * side))
            def _():
                hop(k, side, 0, me).start()

    for k in range(slots):
        tile_copy(k).start()
        raw[k, me] = probe_ref[k]
    for s in range(1, n):
        relay(0, s)
    for k in range(slots):
        if k + 1 < slots:
            relay(k + 1, 1)
        sort_and_send(k)
        if k + 1 < slots:
            for s in range(2, n - 1):
                relay(k + 1, s)
        tile_copy(k).wait()
        backward(k)
        if k + 1 < slots:
            relay(k + 1, n - 1)
    pass_on(0)
    for k in range(slots):
        forward(k)
        if k + 1 < slots:
            pass_on(k + 1)
        combine(k)
    for k in range(slots):
        collect(k)
        sum_inward(k)
        if k > 0:
            send_outward(k - 1)
    send_outward(slots - 1)

    for k in range(slots):
        for side in range(2):
            step = 1 - 2 * side
            for s in range(n - 1):

                @pl.when(inside(me - s * step) & inside(me + step))
                def _():
                    hop(k, side, s, me - s * step).wait_send()

        @pl.when(me > 0)
        def _():
            far_copy(k).wait_send()

        @pl.when(in_row)
        def _():
            for copy in back_copies(k, lax.rem(k + to_wrap, slots)):
                copy.wait_send()

        for e, offset in enumerate(relayed):
            for copy in last_copies(k, e, False):
                copy.wait_send()

            @pl.when(me == offset)
            def _():
                for o in range(n - 1):
                    for copy in mid_copies(k, e, o):
                        copy.wait_send()

        for side in range(2):
            for block in range(n):

                @pl.when(me < block if side == 0 else me > block)
                def _():
                    for copy in own_copies(k, side, block):
                        copy.wait_send()

        gram_across(k).wait_send()

        @pl.when(jnp.logical_not(is_end))
        def _():
            gram_down(k).wait_send()


def reciprocal(value):
    guess = pl.reciprocal(value, approx=True)
    for _ in range(2):
        guess = guess * (2.0 - value * guess)
    return guess


def eliminate(squares):
    parts = NB // 8
    row_at = lax.broadcasted_iota(jnp.int32, (8, 128), 0)
    lane_at = lax.broadcasted_iota(jnp.int32, (8, 128), 1)
    work = [[square[8 * t:8 * t + 8, :] for t in range(parts)] for square in squares]
    unit = [[jnp.where(row_at + 8 * t == lane_at, 1.0, 0.0) for t in range(parts)] for _ in squares]
    for j in range(0, NB, 2):
        top, row = j // 8, j % 8
        for b in range(len(squares)):
            firsts = [jnp.broadcast_to(work[b][t][:, j:j + 1], (8, 128)) for t in range(top, parts)]
            seconds = [jnp.broadcast_to(work[b][t][:, j + 1:j + 2], (8, 128)) for t in range(top, parts)]
            head, cross, tail = firsts[0][row:row + 1], firsts[0][row + 1:row + 2], seconds[0][row + 1:row + 2]
            inverse = reciprocal(head * tail - cross * cross)
            ratio = cross * reciprocal(head)
            tail, cross, head = tail * inverse, cross * inverse, head * inverse
            pairs = [(array[b][top][row:row + 1], array[b][top][row + 1:row + 2]) for array in (work, unit)]
            for t in range(top, parts):
                one = firsts[t - top] * tail - seconds[t - top] * cross
                two = seconds[t - top] * head - firsts[t - top] * cross
                if t == top:
                    one = jnp.where(row_at > row + 1, one, jnp.where(row_at == row + 1, ratio, 0.0))
                    two = jnp.where(row_at > row + 1, two, 0.0)
                for array, (upper, lower) in zip((work, unit), pairs):
                    array[b][t] = array[b][t] - (one * upper + two * lower)
    inverses = []
    for b in range(len(squares)):
        scaled = []
        for t in range(parts):
            pivot = jnp.sum(jnp.where(row_at + 8 * t == lane_at, work[b][t], 0.0), axis=1, keepdims=True)
            scaled.append(unit[b][t] * lax.rsqrt(pivot))
        inverses.append(jnp.concatenate(scaled, axis=0)[:, :NB])
    return inverses


def invert_factors(gram_ref, unit_ref, inverse_ref):
    slots, size = gram_ref.shape[0], gram_ref.shape[1]
    row_at = lax.broadcasted_iota(jnp.int32, (size, size), 0)
    lane_at = lax.broadcasted_iota(jnp.int32, (size, size), 1)
    for k in range(slots):
        unit_ref[k] = jnp.where(row_at == lane_at, 1.0, 0.0)

    def panel(index, carry):
        inverses = eliminate([gram_ref[k, 0:NB, 0:128] for k in range(slots)])
        for k in range(slots):
            across = jnp.dot(inverses[k], gram_ref[k, 0:NB, :], precision=HIGHEST, preferred_element_type=jnp.float32)
            done = jnp.dot(inverses[k], unit_ref[k, 0:NB, :], precision=HIGHEST, preferred_element_type=jnp.float32)
            inverse_ref[k, pl.ds(pl.multiple_of(index * NB, NB), NB), :] = done
            across_t = across.T[NB:, :]
            less = jnp.dot(across_t, across, precision=HIGHEST, preferred_element_type=jnp.float32)
            gram_ref[k, 0:size - NB, :] = pltpu.roll(gram_ref[k, NB:, :] - less, size - NB, 1)
            less = jnp.dot(across_t, done, precision=HIGHEST, preferred_element_type=jnp.float32)
            unit_ref[k, 0:size - NB, :] = unit_ref[k, NB:, :] - less
        return carry

    lax.fori_loop(0, size // NB, panel, 0)


def basis_kernel(points, samples_ref, gram_ref, basis_ref, work_ref, unit_ref, inverse_ref):
    work_ref[...] = gram_ref[...] * (1.0 / points)
    invert_factors(work_ref, unit_ref, inverse_ref)
    for k in range(samples_ref.shape[0]):
        basis_ref[k] = lax.dot_general(
            samples_ref[k], inverse_ref[k], AB_T, precision=HIGHEST, preferred_element_type=jnp.float32
        )


def per_device(tiles, probe, cluster_perm, tile_keep):
    nrows = lax.axis_size("row")
    ncols = lax.axis_size("col")
    slots, points, _ = tiles.shape
    per, width = probe.shape[1:]
    half = width // 2
    relayed = len(range(2, ncols))
    whole = pl.BlockSpec(memory_space=pltpu.VMEM)
    weight = jnp.where(lax.axis_index("col") == 0, 0.5, tile_keep[:, 0, 0].astype(jnp.float32))
    vmem = pltpu.VMEM
    sem = pltpu.SemaphoreType.DMA
    bf16, f32, i16 = jnp.bfloat16, jnp.float32, jnp.int16
    samples, gram_sum = pl.pallas_call(
        functools.partial(samples_kernel, nrows, ncols),
        out_shape=(
            jax.ShapeDtypeStruct((slots, per, width), f32),
            jax.ShapeDtypeStruct((slots, width, width), f32),
        ),
        in_specs=[pl.BlockSpec(memory_space=pltpu.SMEM), pl.BlockSpec(memory_space=pl.ANY), whole, whole],
        out_specs=(whole, whole),
        scratch_shapes=[
            vmem((slots, points, points), bf16),
            vmem((slots, ncols, per, width), bf16),
            vmem((slots, points, width), bf16),
            vmem((slots, points, width), bf16),
            vmem((slots, points, width), i16),
            vmem((slots, 1, points), f32),
            vmem((slots, points, width), i16),
            vmem((slots, 1, points), f32),
            vmem((slots, ncols, per, width), f32),
            vmem((slots, ncols, per, width), i16),
            vmem((slots, ncols, 1, per), f32),
            vmem((slots, 2, ncols, per, width), i16),
            vmem((slots, 2, ncols, 1, per), f32),
            vmem((slots, 3 * half, half), f32),
            vmem((slots, 3 * half, half), f32),
            vmem((slots, 3 * half, half), f32),
            vmem((slots, 3 * half, half), f32),
            vmem((slots, relayed, per, width), i16),
            vmem((slots, relayed, 1, per), f32),
            vmem((slots, relayed, per, width), i16),
            vmem((slots, relayed, 1, per), f32),
            sem((slots,)),
            sem((slots, 2, ncols - 1)),
            sem((slots, 2, ncols - 1)),
            sem((slots,)),
            sem((slots,)),
            sem((slots, 2)),
            sem((slots, 2)),
            sem((slots, ncols, 2)),
            sem((slots, 2, ncols, 2)),
            sem((slots, 2)),
            sem((slots, 2)),
            sem((slots, ncols - 1, 2)),
            sem((slots, relayed, 2)),
            sem((slots, relayed, 2)),
            sem((slots, relayed, 2)),
        ],
        compiler_params=pltpu.CompilerParams(vmem_limit_bytes=LIMIT, collective_id=0, has_side_effects=True),
        cost_estimate=pl.CostEstimate(
            flops=12 * slots * points * points * width, bytes_accessed=2 * tiles.size, transcendentals=0
        ),
        name="samples",
    )(weight, tiles, probe, cluster_perm)
    square = vmem((slots, width, width), f32)
    leaf_basis = pl.pallas_call(
        functools.partial(basis_kernel, points),
        out_shape=jax.ShapeDtypeStruct(samples.shape, f32),
        in_specs=[whole, whole],
        out_specs=whole,
        scratch_shapes=[square, square, square],
        compiler_params=pltpu.CompilerParams(vmem_limit_bytes=LIMIT),
        name="leaf_basis",
    )(samples, gram_sum)
    return (samples, leaf_basis)


def solution(mesh):
    placed = (
        P(None, "row", "col"),
        P(None, ("row", "col"), None),
        P(None, "row", None),
        P(None, "row", "col"),
    )
    return jax.shard_map(
        per_device,
        mesh=mesh,
        in_specs=placed,
        out_specs=(P(None, ("row", "col"), None), P(None, ("row", "col"), None)),
        check_vma=False,
    )
```
